32 devices in a mesh: grp: 2 (over y), rows: 8 (over z, x), cols: 2 (over core).
Axes of the slice: x: 2, y: 2, z: 4, core: 2. Of those that a mesh axis runs over, the one named last changes fastest.
Arguments:
- masks: bfloat16 [2560, 25088], P(('grp', 'rows'), 'cols'), parts along dimension 0, may hold values from 0 to 1, as said below
- targets: float32 [2, 2560, 40], P(None, ('grp', 'rows')), parts along dimension 1, may hold values from -6 to 6
- weights_in: float32 [80, 25088], P('grp', ('cols', 'rows')), parts along dimension 0, may hold values from -5 to 5
- bias_in: float32 [80], P('grp'), parts along dimension 0, may hold values from -5 to 5
- threshold: float32 [80], P('grp'), parts along dimension 0, may hold values from 0.05 to 0.4
- live_pairs: int32 [16], P(('grp', 'rows')), parts along dimension 0, may hold values from 40 to 160, as said below
Outputs:
- weights: float32 [80, 25088], P('grp', ('cols', 'rows')), parts along dimension 0
- bias: float32 [80], P('grp'), parts along dimension 0
- residual: float32 [2, 2560, 40], P(None, ('grp', 'rows')), parts along dimension 1
The draws below stay inside these ranges and needn't reach their ends.
There are 2 independent parts, one for each index of `grp`. The reference program is written for one: setup_inputs(seed, part) draws one part's arguments, and reference() takes and returns one part's arrays. A program takes and returns all parts, laid end to end along the dimension named above; each array names one. Nothing has to cross between parts.
Inputs may be any that keep to these rules, and one draw needn't show every extreme that they name: `masks`: each entry is 0 or 1. `live_pairs`: A device's live pairs are its first slots; in every draw some device has all 160 slots live.
All inputs are finite; a program needn't handle non-finite values.
Results may differ from the reference program's by a relative error of at most 0.0052.
Values may be sent and summed in bfloat16 or wider, within the bound.
A program may use at most 64 MiB of HBM per device.

```python
import math
import jax
import jax.numpy as jnp
from jax import lax

N = 25088
K = 40
HP = 160
ITERS = 2
MP = 1280
N_ROWS = 8


def draw_masks(key, part):
    key = jax.random.fold_in(key, 11)
    bits = jax.random.randint(key, (MP, N), 0, 2)
    return bits.astype(jnp.float32).astype(jnp.bfloat16)


def draw_live_pairs(key, part):
    key = jax.random.fold_in(key, 23)
    first, second = jax.random.split(key)
    counts = jax.random.randint(first, (N_ROWS,), max(1, HP // 4), HP + 1)
    full = jax.random.randint(second, (), 0, N_ROWS)
    place = jnp.arange(N_ROWS, dtype=jnp.int32)
    return jnp.where(place == full, HP, counts).astype(jnp.int32)


def level_of(key, dims, pieces, low, largest):
    gain, own = 1.0, jax.random.fold_in(key, 6)
    for dim, blocks in pieces:
        draws = jnp.exp(jax.random.uniform(jax.random.fold_in(own, dim), (blocks,), jnp.float32, low / len(pieces), largest / len(pieces)))
        gain = gain * jnp.repeat(draws, dims[dim] // blocks).reshape([-1 if axis == dim else 1 for axis in range(len(dims))])
    return gain


def normal_values(rng, shape, scale, limit, cuts=(), held_as=jnp.bfloat16):
    level = level_of(rng, shape, cuts, -0.22, 0.18) if cuts else 1.0
    values = jax.random.normal(rng, shape, jnp.float32) * scale * level
    return jnp.minimum(jnp.maximum(values, -limit), limit).astype(held_as)


def setup_inputs(seed: int = 0, part: int = 0) -> dict:
    streams_of = jax.random.split(jax.random.key(seed), 7)
    part_keys = jax.random.split(jax.random.fold_in(streams_of[6], part), 7)
    masks = draw_masks(jax.random.fold_in(jax.random.fold_in(streams_of[6], part), 71), part)
    targets = normal_values(part_keys[1], (2, MP, K), 1.0, 6.0, ((1, 8),), jnp.float32)
    weights_in = normal_values(part_keys[2], (K, N), 1.0, 5.0, ((1, 16),), jnp.float32)
    bias_in = normal_values(part_keys[3], (K,), 1.0, 5.0, (), jnp.float32)
    threshold = jnp.clip(jnp.exp(jax.random.uniform(part_keys[4], (K,), jnp.float32, math.log(0.05), math.log(0.4))), 0.05, 0.4)
    live_pairs = draw_live_pairs(jax.random.fold_in(jax.random.fold_in(streams_of[6], part), 71), part)
    return dict(masks=masks, targets=targets, weights_in=weights_in, bias_in=bias_in, threshold=threshold, live_pairs=live_pairs)


def shrink(values, threshold):
    bound = threshold[:, None]
    return values - jnp.clip(values, -bound, bound)

def reference(masks, targets, weights_in, bias_in, threshold, live_pairs):
    scale = 1.0 / math.sqrt(N)
    slot = jnp.arange(HP, dtype=jnp.int32)
    live = (slot[None, :] < live_pairs[:, None]).astype(jnp.float32).reshape(N_ROWS * HP, 1)
    count = 2.0 * jnp.sum(live_pairs.astype(jnp.float32))
    factor = 0.2 * N * scale / count
    blocks = masks.reshape(N_ROWS, HP, N)
    weights = weights_in
    bias = bias_in
    upper = None
    lower = None
    for iteration in range(ITERS + 1):
        block16 = weights.astype(jnp.bfloat16)

        def score(piece):
            signed = piece * 2 - 1
            return lax.dot_general(signed, block16, (((1,), (1,)), ((), ())), preferred_element_type=jnp.float32)
        scores = lax.map(score, blocks).reshape(N_ROWS * HP, K) * scale
        upper = live * (scores + bias - targets[0])
        lower = live * (-scores + bias - targets[1])
        if iteration < ITERS:
            stacked = jnp.concatenate([upper.astype(jnp.bfloat16), lower.astype(jnp.bfloat16)], 1)
            stacked = stacked.reshape(N_ROWS, HP, 2 * K)

            def accumulate(total, item):
                piece, resid = item
                signed = piece * 2 - 1
                term = lax.dot_general(resid, signed, (((0,), (0,)), ((), ())), preferred_element_type=jnp.float32)
                return (total + term, None)
            both, unused = lax.scan(accumulate, jnp.zeros((2 * K, N), jnp.float32), (blocks, stacked))
            raw = both[:K] - both[K:]
            bias_sum = lax.optimization_barrier(jnp.sum(upper + lower, 0))
            weights = shrink(weights - factor * raw, threshold)
            bias = bias - 0.5 * bias_sum / count
    residual = jnp.stack([upper, lower], 0)
    return (weights, bias, residual)
```

```python
import functools
import math

import jax
import jax.numpy as jnp
from jax import lax
from jax.experimental import pallas as pl
from jax.experimental.pallas import tpu as pltpu
from jax.sharding import PartitionSpec as P

N = 25088
ITERS = 2
LANES = 128
F32 = jnp.float32
BF16 = jnp.bfloat16


def shrink(values, bound):
    return values - jnp.clip(values, -bound, bound)


def plain(masks, targets, weights_in, bias_in, threshold, live_pairs):
    slots = masks.shape[0]
    scale = 1.0 / math.sqrt(N)
    live = (lax.broadcasted_iota(jnp.int32, (slots, 1), 0) < live_pairs[0]).astype(F32)
    count = 2.0 * lax.psum(live_pairs[0].astype(F32), "rows")
    factor = 0.2 * N * scale / count
    signed = masks * 2 - 1
    bias = bias_in
    share = weights_in.shape[1]
    whole = lax.all_gather(weights_in, "rows", axis=1, tiled=True)
    for iteration in range(ITERS + 1):
        part = lax.dot_general(
            signed, whole.astype(BF16), (((1,), (1,)), ((), ())), preferred_element_type=F32
        )
        total = lax.psum(part, "cols") * scale
        upper = live * (total + bias - targets[0])
        lower = live * (-total + bias - targets[1])
        if iteration < ITERS:
            stacked = jnp.concatenate([upper.astype(BF16), lower.astype(BF16)], 1)
            both = lax.dot_general(
                stacked, signed, (((0,), (0,)), ((), ())), preferred_element_type=F32
            )
            k = upper.shape[1]
            raw, bias_sum = lax.psum((both[:k] - both[k:], jnp.sum(upper + lower, 0)), "rows")
            whole = shrink(whole - factor * raw, threshold[:, None])
            bias = bias - 0.5 * bias_sum / count
    weights = lax.dynamic_slice_in_dim(whole, lax.axis_index("rows") * share, share, 1)
    return weights, bias, jnp.stack([upper, lower], 0)


def body(
    tiles, nz,
    masks_hbm, targets, w_in, bias_in, thr, live_pairs,
    w_out, b_out, res_out,
    sm, wf, ag, xs, xr, zs, zr, bs, br, ss, sr,
    mask_sem, own_send, fwd_send, z_recv, x_recv,
    xs_send, xs_recv, zs_send, zs_recv, b_send, b_recv, s_send, s_recv,
):
    k_rows, share = w_in.shape
    slots = sm.shape[0]
    win = tiles * LANES
    half = (tiles + 1) // 2 * LANES
    tail = win - half
    scale = 1.0 / math.sqrt(N)

    r = lax.axis_index("rows")
    c = lax.axis_index("cols")
    z = r // 2
    x = r % 2
    xpeer = z * 2 + (1 - x)

    def owner(k, other):
        zk = lax.rem(z + k, nz)
        return zk * 2 + ((1 - x) if other else x)

    def sender_to(k, other):
        zk = lax.rem(z + (nz - k), nz)
        return zk * 2 + ((1 - x) if other else x)

    def start_of(o):
        return pl.multiple_of((o * share) // LANES * LANES, LANES)

    offset = r * share - (r * share) // LANES * LANES

    mask_copy = pltpu.make_async_copy(masks_hbm, sm, mask_sem)
    mask_copy.start()

    barrier = pltpu.get_barrier_semaphore()
    for k in range(nz):
        for other in (0, 1):
            if k or other:
                pl.semaphore_signal(
                    barrier, inc=1, device_id={"rows": owner(k, other)},
                    device_id_type=pl.DeviceIdType.MESH,
                )
    pl.semaphore_signal(
        barrier, inc=1, device_id={"cols": 1 - c}, device_id_type=pl.DeviceIdType.MESH
    )

    pending = []

    def send(src, dst, ssem, rsem, where):
        copy = pltpu.make_async_remote_copy(
            src_ref=src, dst_ref=dst, send_sem=ssem, recv_sem=rsem,
            device_id=where, device_id_type=pl.DeviceIdType.MESH,
        )
        copy.start()
        pending.append(copy)
        return copy

    def pack(value, ref):
        ref[:, 0:win] = value[0:16].astype(BF16)
        ref[:, win : 2 * win] = value[16:32].astype(BF16)
        last = value[32:40]
        ref[:, 2 * win : 2 * win + half] = jnp.concatenate(
            [last[:, :half], last[:, win - half :]], 0
        ).astype(BF16)

    def unpack(ref):
        both = ref[:, 2 * win : 2 * win + half].astype(F32)
        last = jnp.concatenate([both[:8], both[8:, half - tail :]], 1)
        return jnp.concatenate(
            [ref[:, 0:win].astype(F32), ref[:, win : 2 * win].astype(F32), last], 0
        )

    lane = lax.broadcasted_iota(jnp.int32, (1, win), 1)
    mine = (lane >= offset) & (lane < offset + share)
    wf[:, 0:share] = w_in[...]
    wf[:, share:win] = jnp.zeros((k_rows, win - share), F32)
    wf[...] = pltpu.roll(wf[...], offset, 1)
    pack(wf[...], ag.at[0, 0, 0])

    pl.semaphore_wait(barrier, 2 * nz)

    def send_own(t):
        own = ag.at[t, 0, 0]
        send(own, ag.at[t, 0, 1], own_send.at[t, 0], x_recv.at[t, 0], {"rows": xpeer})
        for k in range(1, nz):
            send(own, ag.at[t, k, 0], own_send.at[t, k], z_recv.at[t, k], {"rows": sender_to(k, 0)})

    def window_scores(t, k, other):
        block = unpack(ag.at[t, k, other]).astype(BF16)
        start = start_of(owner(k, other))
        return lax.dot_general(
            block, sm[:, pl.ds(start, win)], (((1,), (1,)), ((), ())), preferred_element_type=F32
        )

    def recv(dst, rsem):
        pltpu.make_async_copy(dst, dst, rsem).wait()

    send_own(0)
    mask_copy.wait()
    for i in range(slots // 16):
        rows = pl.ds(i * 16, 16)
        sm[rows, :] = sm[rows, :] * 2 - 1

    live = (lax.broadcasted_iota(jnp.int32, (1, slots), 1) < live_pairs[0]).astype(F32)
    eye = (
        lax.broadcasted_iota(jnp.int32, (k_rows, LANES), 0)
        == lax.broadcasted_iota(jnp.int32, (k_rows, LANES), 1)
    ).astype(F32)
    last_lane = lax.broadcasted_iota(jnp.int32, (1, LANES), 1) == LANES - 1
    bias = bias_in[...]
    bound = thr[...]

    def gradient(stacked, k, other):
        start = start_of(owner(k, other))
        both = jnp.dot(stacked, sm[:, pl.ds(start, win)], preferred_element_type=F32)
        return both[:k_rows] - both[k_rows:]

    for t in range(ITERS + 1):
        part = window_scores(t, 0, 0)
        for k in range(1, nz):
            recv(ag.at[t, k, 0], z_recv.at[t, k])
            send(ag.at[t, k, 0], ag.at[t, k, 1], fwd_send.at[t, k], x_recv.at[t, k], {"rows": xpeer})
            part += window_scores(t, k, 0)
        for k in range(nz):
            recv(ag.at[t, k, 1], x_recv.at[t, k])
            part += window_scores(t, k, 1)

        ss[t] = part
        copy = send(ss.at[t], sr.at[t], s_send.at[t], s_recv.at[t], {"cols": 1 - c})
        copy.wait_recv()
        total = (part + sr[t]) * scale
        upper = live * (total + bias - targets[0])
        lower = live * (-total + bias - targets[1])
        if t == ITERS:
            res_out[0] = upper
            res_out[1] = lower
            break

        stacked = jnp.concatenate([upper, lower], 0).astype(BF16)
        order = list(range(1, nz)) + [0]
        for k in order:
            pack(gradient(stacked, k, 1), xs.at[t, k])
            send(xs.at[t, k], xr.at[t, k], xs_send.at[t, k], xs_recv.at[t, k], {"rows": xpeer})

        column = jnp.sum(upper + lower, 1, keepdims=True)
        row = jnp.sum(column * eye, 0, keepdims=True)
        row = jnp.where(last_lane, live_pairs[0].astype(F32), row)
        bs[t] = jnp.broadcast_to(row, (8, LANES))
        br[t, r] = jnp.broadcast_to(row, (8, LANES))
        for k in range(nz):
            for other in (0, 1):
                if k or other:
                    send(
                        bs.at[t], br.at[t, r], b_send.at[t, k, other], b_recv.at[t, k, other],
                        {"rows": sender_to(k, other)},
                    )

        for k in range(1, nz):
            own = gradient(stacked, k, 0)
            recv(xr.at[t, k], xs_recv.at[t, k])
            pack(own + unpack(xr.at[t, k]), zs.at[t, k])
            send(zs.at[t, k], zr.at[t, k], zs_send.at[t, k], zs_recv.at[t, k], {"rows": owner(k, 0)})
        raw = gradient(stacked, 0, 0)
        recv(xr.at[t, 0], xs_recv.at[t, 0])
        raw += unpack(xr.at[t, 0])

        for k in range(nz):
            for other in (0, 1):
                if k or other:
                    recv(br.at[t, owner(k, other)], b_recv.at[t, k, other])
        sums = br[t, 0]
        for j in range(1, 2 * nz):
            sums += br[t, j]
        sums = sums[0:1]
        count = 2.0 * jnp.sum(jnp.where(last_lane, sums, 0.0), 1, keepdims=True)
        bias_sum = jnp.sum(sums * eye, 1, keepdims=True)
        factor = 0.2 * N * scale / count
        bias = bias - 0.5 * bias_sum / count

        for k in range(1, nz):
            recv(zr.at[t, k], zs_recv.at[t, k])
            raw += unpack(zr.at[t, k])
        new = jnp.where(mine, shrink(wf[...] - factor * raw, bound), 0.0)
        wf[...] = new
        pack(new, ag.at[t + 1, 0, 0])
        send_own(t + 1)

    b_out[...] = bias
    w_out[...] = pltpu.roll(wf[...], lax.rem(win - offset, win), 1)[:, :share]
    for copy in pending:
        copy.wait_send()


def fused(rows, masks, targets, weights_in, bias_in, threshold, live_pairs):
    slots, cols = masks.shape
    k_rows, share = weights_in.shape
    nz = rows // 2
    tiles = max(-(-share * (j + 1) // LANES) - share * j // LANES for j in range(rows))
    packed = (16, 2 * tiles * LANES + (tiles + 1) // 2 * LANES)
    turns = ITERS + 1
    dma = pltpu.SemaphoreType.DMA
    vmem = pl.BlockSpec(memory_space=pltpu.VMEM)
    weights, bias, residual = pl.pallas_call(
        functools.partial(body, tiles, nz),
        out_shape=(
            jax.ShapeDtypeStruct((k_rows, share), F32),
            jax.ShapeDtypeStruct((k_rows, 1), F32),
            jax.ShapeDtypeStruct((2, k_rows, slots), F32),
        ),
        in_specs=[
            pl.BlockSpec(memory_space=pl.ANY), vmem, vmem, vmem, vmem,
            pl.BlockSpec(memory_space=pltpu.SMEM),
        ],
        out_specs=(vmem, vmem, vmem),
        scratch_shapes=[
            pltpu.VMEM((slots, cols), BF16),
            pltpu.VMEM((k_rows, tiles * LANES), F32),
            pltpu.VMEM((turns, nz, 2) + packed, BF16),
            pltpu.VMEM((ITERS, nz) + packed, BF16),
            pltpu.VMEM((ITERS, nz) + packed, BF16),
            pltpu.VMEM((ITERS, nz) + packed, BF16),
            pltpu.VMEM((ITERS, nz) + packed, BF16),
            pltpu.VMEM((ITERS, 8, LANES), F32),
            pltpu.VMEM((ITERS, rows, 8, LANES), F32),
            pltpu.VMEM((turns, k_rows, slots), F32),
            pltpu.VMEM((turns, k_rows, slots), F32),
            dma,
            dma((turns, nz)), dma((turns, nz)), dma((turns, nz)), dma((turns, nz)),
            dma((ITERS, nz)), dma((ITERS, nz)), dma((ITERS, nz)), dma((ITERS, nz)),
            dma((ITERS, nz, 2)), dma((ITERS, nz, 2)),
            dma((turns,)), dma((turns,)),
        ],
        compiler_params=pltpu.CompilerParams(
            collective_id=0, has_side_effects=True, vmem_limit_bytes=48 * 1024 * 1024
        ),
    )(
        masks, jnp.swapaxes(targets, 1, 2), weights_in,
        bias_in[:, None], threshold[:, None], live_pairs,
    )
    return weights, bias[:, 0], jnp.swapaxes(residual, 1, 2)


def solution(mesh):
    rows = mesh.shape["rows"]
    on_device = functools.partial(fused, rows) if rows == 8 else plain
    return jax.shard_map(
        on_device,
        mesh=mesh,
        in_specs=(
            P(("grp", "rows"), "cols"),
            P(None, ("grp", "rows"), None),
            P("grp", ("cols", "rows")),
            P("grp"),
            P("grp"),
            P(("grp", "rows")),
        ),
        out_specs=(P("grp", ("cols", "rows")), P("grp"), P(None, ("grp", "rows"), None)),
        check_vma=False,
    )
```

```python
import functools
import math

import jax
import jax.numpy as jnp
from jax import lax
from jax.experimental import pallas as pl
from jax.experimental.pallas import tpu as pltpu
from jax.sharding import PartitionSpec as P

N = 25088
ITERS = 2
LANES = 128
F32 = jnp.float32
BF16 = jnp.bfloat16


def shrink(values, bound):
    return values - jnp.clip(values, -bound, bound)


def plain(masks, targets, weights_in, bias_in, threshold, live_pairs):
    slots = masks.shape[0]
    scale = 1.0 / math.sqrt(N)
    live = (lax.broadcasted_iota(jnp.int32, (slots, 1), 0) < live_pairs[0]).astype(F32)
    count = 2.0 * lax.psum(live_pairs[0].astype(F32), "rows")
    factor = 0.2 * N * scale / count
    signed = masks * 2 - 1
    bias = bias_in
    share = weights_in.shape[1]
    whole = lax.all_gather(weights_in, "rows", axis=1, tiled=True)
    for iteration in range(ITERS + 1):
        part = lax.dot_general(
            signed, whole.astype(BF16), (((1,), (1,)), ((), ())), preferred_element_type=F32
        )
        total = lax.psum(part, "cols") * scale
        upper = live * (total + bias - targets[0])
        lower = live * (-total + bias - targets[1])
        if iteration < ITERS:
            stacked = jnp.concatenate([upper.astype(BF16), lower.astype(BF16)], 1)
            both = lax.dot_general(
                stacked, signed, (((0,), (0,)), ((), ())), preferred_element_type=F32
            )
            k = upper.shape[1]
            raw, bias_sum = lax.psum((both[:k] - both[k:], jnp.sum(upper + lower, 0)), "rows")
            whole = shrink(whole - factor * raw, threshold[:, None])
            bias = bias - 0.5 * bias_sum / count
    weights = lax.dynamic_slice_in_dim(whole, lax.axis_index("rows") * share, share, 1)
    return weights, bias, jnp.stack([upper, lower], 0)


GROUPS = ((0, 24), (24, 16))
LEAD = 1
PER_GROUP = 22


def folded(size, tiles):
    return size // 16 * tiles * LANES + size % 16 // 8 * ((tiles + 1) // 2) * LANES


def body(
    tiles, nz,
    masks_hbm, targets_hbm, w_hbm, bias_in, thr, live_pairs,
    w_out, b_out, res_out,
    sm, wf, w_in, targets, mask_sem, w_sem, targets_sem, *per_group,
):
    k_rows, share = w_in.shape
    slots = sm.shape[0]
    win = tiles * LANES
    half = (tiles + 1) // 2 * LANES
    tail = win - half
    scale = 1.0 / math.sqrt(N)

    r = lax.axis_index("rows")
    c = lax.axis_index("cols")
    z = r // 2
    x = r % 2
    xpeer = z * 2 + (1 - x)

    def owner(k, other):
        zk = lax.rem(z + k, nz)
        return zk * 2 + ((1 - x) if other else x)

    def sender_to(k, other):
        zk = lax.rem(z + (nz - k), nz)
        return zk * 2 + ((1 - x) if other else x)

    def start_of(o):
        return pl.multiple_of((o * share) // LANES * LANES, LANES)

    offset = r * share - (r * share) // LANES * LANES

    w_copy = pltpu.make_async_copy(w_hbm, w_in, w_sem)
    w_copy.start()
    mask_copy = pltpu.make_async_copy(masks_hbm, sm, mask_sem)
    mask_copy.start()
    targets_copy = pltpu.make_async_copy(targets_hbm, targets, targets_sem)
    targets_copy.start()

    barrier = pltpu.get_barrier_semaphore()
    for k in range(nz):
        for other in (0, 1):
            if k or other:
                pl.semaphore_signal(
                    barrier, inc=1, device_id={"rows": owner(k, other)},
                    device_id_type=pl.DeviceIdType.MESH,
                )
    pl.semaphore_signal(
        barrier, inc=1, device_id={"cols": 1 - c}, device_id_type=pl.DeviceIdType.MESH
    )

    pending = []

    def send(src, dst, ssem, rsem, where):
        copy = pltpu.make_async_remote_copy(
            src_ref=src, dst_ref=dst, send_sem=ssem, recv_sem=rsem,
            device_id=where, device_id_type=pl.DeviceIdType.MESH,
        )
        copy.start()
        pending.append(copy)
        return copy

    def recv(dst, rsem):
        pltpu.make_async_copy(dst, dst, rsem).wait()

    def pack(value, ref):
        at = 0
        for top in range(0, value.shape[0] // 16 * 16, 16):
            ref[:, at : at + win] = value[top : top + 16].astype(BF16)
            at += win
        if value.shape[0] % 16:
            last = value[-8:]
            ref[:, at : at + half] = jnp.concatenate(
                [last[:, :half], last[:, win - half :]], 0
            ).astype(BF16)

    def unpack(ref, size):
        parts = []
        at = 0
        for top in range(0, size // 16 * 16, 16):
            parts.append(ref[:, at : at + win].astype(F32))
            at += win
        if size % 16:
            both = ref[:, at : at + half].astype(F32)
            parts.append(jnp.concatenate([both[:8], both[8:, half - tail :]], 1))
        return jnp.concatenate(parts, 0) if len(parts) > 1 else parts[0]

    lane = lax.broadcasted_iota(jnp.int32, (1, win), 1)
    mine = (lane >= offset) & (lane < offset + share)
    w_copy.wait()
    wf[:, 0:share] = w_in[...]
    wf[:, share:win] = jnp.zeros((k_rows, win - share), F32)
    wf[...] = pltpu.roll(wf[...], offset, 1)

    def send_own(g, t):
        (ag, *_, own_send, _, z_recv, x_recv) = per_group[g * PER_GROUP : g * PER_GROUP + 13]
        top, size = GROUPS[g]
        own = ag.at[t, 0, 0]
        pack(wf[top : top + size], own)
        for k in range(1, nz):
            send(own, ag.at[t, k, 0], own_send.at[t, k], z_recv.at[t, k], {"rows": sender_to(k, 0)})
        send(own, ag.at[t, 0, 1], own_send.at[t, 0], x_recv.at[t, 0], {"rows": xpeer})

    live = (lax.broadcasted_iota(jnp.int32, (1, slots), 1) < live_pairs[0]).astype(F32)
    last_lane = lax.broadcasted_iota(jnp.int32, (1, LANES), 1) == LANES - 1

    def chain(g):
        (
            ag, xs, xr, zs, zr, bs, br, ss, sr,
            own_send, fwd_send, z_recv, x_recv,
            xs_send, xs_recv, zs_send, zs_recv, b_send, b_recv, s_send, s_recv, counted,
        ) = per_group[g * PER_GROUP : (g + 1) * PER_GROUP]
        top, size = GROUPS[g]
        mid = slice(top, top + size)
        pick = (
            lax.broadcasted_iota(jnp.int32, (size, k_rows), 0) + top
            == lax.broadcasted_iota(jnp.int32, (size, k_rows), 1)
        ).astype(F32)
        eye = (
            lax.broadcasted_iota(jnp.int32, (size, LANES), 0)
            == lax.broadcasted_iota(jnp.int32, (size, LANES), 1)
        ).astype(F32)
        bias = jnp.sum(pick * bias_in[...], 1, keepdims=True)
        bound = jnp.sum(pick * thr[...], 1, keepdims=True)

        def window_scores(t, k, other):
            block = unpack(ag.at[t, k, other], size).astype(BF16)
            start = start_of(owner(k, other))
            return lax.dot_general(
                block, sm[:, pl.ds(start, win)], (((1,), (1,)), ((), ())),
                preferred_element_type=F32,
            )

        def gradient(stacked, k, other):
            start = start_of(owner(k, other))
            both = jnp.dot(stacked, sm[:, pl.ds(start, win)], preferred_element_type=F32)
            return both[:size] - both[size:]

        for t in range(ITERS + 1):
            part = window_scores(t, 0, 0)
            for k in range(1, nz):
                recv(ag.at[t, k, 0], z_recv.at[t, k])
                send(
                    ag.at[t, k, 0], ag.at[t, k, 1], fwd_send.at[t, k], x_recv.at[t, k],
                    {"rows": xpeer},
                )
                part += window_scores(t, k, 0)
            yield
            for k in range(nz):
                recv(ag.at[t, k, 1], x_recv.at[t, k])
                part += window_scores(t, k, 1)
            ss[t] = part
            copy = send(ss.at[t], sr.at[t], s_send.at[t], s_recv.at[t], {"cols": 1 - c})
            yield
            copy.wait_recv()
            total = (ss[t] + sr[t]) * scale
            upper = live * (total + bias - targets[0, mid])
            lower = live * (-total + bias - targets[1, mid])
            if t == ITERS:
                res_out[0, mid] = upper
                res_out[1, mid] = lower
                counted[...] = jnp.broadcast_to(jnp.sum(pick * bias, 0, keepdims=True), counted.shape)
                return

            stacked = jnp.concatenate([upper, lower], 0).astype(BF16)
            for k in list(range(1, nz)) + [0]:
                pack(gradient(stacked, k, 1), xs.at[t, k])
                send(xs.at[t, k], xr.at[t, k], xs_send.at[t, k], xs_recv.at[t, k], {"rows": xpeer})

            column = jnp.sum(upper + lower, 1, keepdims=True)
            row = jnp.sum(column * eye, 0, keepdims=True)
            row = jnp.where(last_lane, live_pairs[0].astype(F32), row)
            bs[t] = jnp.broadcast_to(row, (8, LANES))
            br[t, r] = jnp.broadcast_to(row, (8, LANES))
            for k in range(nz):
                for other in (0, 1):
                    if k or other:
                        send(
                            bs.at[t], br.at[t, r], b_send.at[t, k, other], b_recv.at[t, k, other],
                            {"rows": sender_to(k, other)},
                        )
            yield

            for k in range(1, nz):
                own = gradient(stacked, k, 0)
                recv(xr.at[t, k], xs_recv.at[t, k])
                pack(own + unpack(xr.at[t, k], size), zs.at[t, k])
                send(
                    zs.at[t, k], zr.at[t, k], zs_send.at[t, k], zs_recv.at[t, k],
                    {"rows": owner(k, 0)},
                )
            yield

            raw = gradient(stacked, 0, 0)
            recv(xr.at[t, 0], xs_recv.at[t, 0])
            raw += unpack(xr.at[t, 0], size)
            for k in range(nz):
                for other in (0, 1):
                    if k or other:
                        recv(br.at[t, owner(k, other)], b_recv.at[t, k, other])
            sums = br[t, 0]
            for j in range(1, 2 * nz):
                sums += br[t, j]
            sums = sums[0:1]
            count = 2.0 * jnp.sum(jnp.where(last_lane, sums, 0.0), 1, keepdims=True)
            bias_sum = jnp.sum(sums * eye, 1, keepdims=True)
            factor = 0.2 * N * scale / count
            bias = bias - 0.5 * bias_sum / count
            for k in range(1, nz):
                recv(zr.at[t, k], zs_recv.at[t, k])
                raw += unpack(zr.at[t, k], size)
            wf[mid] = jnp.where(mine, shrink(wf[mid] - factor * raw, bound), 0.0)
            send_own(g, t + 1)
            yield

    pl.semaphore_wait(barrier, 2 * nz)
    for g in range(len(GROUPS)):
        send_own(g, 0)
    mask_copy.wait()
    targets_copy.wait()
    for i in range(slots // 16):
        rows = pl.ds(i * 16, 16)
        sm[rows, :] = sm[rows, :] * 2 - 1

    chains = [chain(g) for g in range(len(GROUPS))]
    for ahead in range(LEAD):
        next(chains[0], None)
    turn = 1
    alive = set(range(len(chains)))
    while alive:
        g = turn % len(chains)
        turn += 1
        if g in alive:
            try:
                next(chains[g])
            except StopIteration:
                alive.remove(g)

    final = sum(per_group[g * PER_GROUP + PER_GROUP - 1][0:1] for g in range(len(GROUPS)))
    b_out[...] = final
    w_out[...] = pltpu.roll(wf[...], lax.rem(win - offset, win), 1)[:, :share]
    for copy in pending:
        copy.wait_send()


def fused(rows, masks, targets, weights_in, bias_in, threshold, live_pairs):
    slots, cols = masks.shape
    k_rows, share = weights_in.shape
    nz = rows // 2
    tiles = max(-(-share * (j + 1) // LANES) - share * j // LANES for j in range(rows))
    turns = ITERS + 1
    dma = pltpu.SemaphoreType.DMA
    vmem = pl.BlockSpec(memory_space=pltpu.VMEM)
    hbm = pl.BlockSpec(memory_space=pltpu.HBM)
    per_group = []
    for top, size in GROUPS:
        packed = (16, folded(size, tiles))
        mine = [
            pltpu.VMEM((turns, nz, 2) + packed, BF16),
            pltpu.VMEM((ITERS, nz) + packed, BF16),
            pltpu.VMEM((ITERS, nz) + packed, BF16),
            pltpu.VMEM((ITERS, nz) + packed, BF16),
            pltpu.VMEM((ITERS, nz) + packed, BF16),
            pltpu.VMEM((ITERS, 8, LANES), F32),
            pltpu.VMEM((ITERS, rows, 8, LANES), F32),
            pltpu.VMEM((turns, size, slots), F32),
            pltpu.VMEM((turns, size, slots), F32),
            dma((turns, nz)), dma((turns, nz)), dma((turns, nz)), dma((turns, nz)),
            dma((ITERS, nz)), dma((ITERS, nz)), dma((ITERS, nz)), dma((ITERS, nz)),
            dma((ITERS, nz, 2)), dma((ITERS, nz, 2)),
            dma((turns,)), dma((turns,)),
            pltpu.VMEM((8, k_rows), F32),
        ]
        per_group += mine
    weights, bias, residual = pl.pallas_call(
        functools.partial(body, tiles, nz),
        out_shape=(
            jax.ShapeDtypeStruct((k_rows, share), F32),
            jax.ShapeDtypeStruct((1, k_rows), F32),
            jax.ShapeDtypeStruct((2, k_rows, slots), F32),
        ),
        in_specs=[
            hbm, hbm, hbm, vmem, vmem,
            pl.BlockSpec(memory_space=pltpu.SMEM),
        ],
        out_specs=(vmem, vmem, vmem),
        scratch_shapes=[
            pltpu.VMEM((slots, cols), BF16),
            pltpu.VMEM((k_rows, tiles * LANES), F32),
            pltpu.VMEM((k_rows, share), F32),
            pltpu.VMEM((2, k_rows, slots), F32),
            dma, dma, dma,
        ] + per_group,
        compiler_params=pltpu.CompilerParams(
            collective_id=0, has_side_effects=True, vmem_limit_bytes=48 * 1024 * 1024
        ),
    )(
        masks, jnp.swapaxes(targets, 1, 2), weights_in,
        bias_in[None], threshold[None], live_pairs,
    )
    return weights, bias[0], jnp.swapaxes(residual, 1, 2)


def solution(mesh):
    rows = mesh.shape["rows"]
    on_device = functools.partial(fused, rows) if rows == 8 else plain
    return jax.shard_map(
        on_device,
        mesh=mesh,
        in_specs=(
            P(("grp", "rows"), "cols"),
            P(None, ("grp", "rows"), None),
            P("grp", ("cols", "rows")),
            P("grp"),
            P("grp"),
            P(("grp", "rows")),
        ),
        out_specs=(P("grp", ("cols", "rows")), P("grp"), P(None, ("grp", "rows"), None)),
        check_vma=False,
    )
```
